32 devices in a mesh: ctx: 8 (over y, x, core), tp: 4 (over z).
Axes of the slice: x: 2, y: 2, z: 4, core: 2. Of those that a mesh axis runs over, the one named last changes fastest.
Arguments:
- rotated_queries: bfloat16 [4096, 8192], P('ctx', 'tp'), may hold values from -25 to 25
- rotated_keys: bfloat16 [4096, 1024], P('ctx', 'tp'), may hold values from -25 to 25
- value_matrix: bfloat16 [4096, 1024], P('ctx', 'tp'), may hold values from -6 to 6
- out_weight: bfloat16 [8192, 8192], P('tp', 'ctx'), may hold values from -0.0625 to 0.0625
- doc_ids: int32 [4096], replicated, may hold values from 0 to 3, never falling along the last dimension, each value on 1 to 2048 neighbouring positions
- assignment: int32 [8, 8], replicated, may hold values from 0 to 7, each once within a row
Outputs:
- owner_output: bfloat16 [4096, 8192], P('ctx', 'tp')
The draws below stay inside these ranges and needn't reach their ends.
Inputs may be any that keep to these rules, and one draw needn't show every extreme that they name: Each row of assignment is a permutation of 0 to 7. `doc_ids`: documents are numbered in order along the tokens; each has 1 to 2048 tokens and one has exactly 2048.
All inputs are finite; a program needn't handle non-finite values.
Results may differ from the reference program's by a relative error of at most 0.017.
Values may be sent and summed in bfloat16 or wider, within the bound.
A program may use at most 320 MiB of HBM per device.

```python
import math
import jax
import jax.numpy as jnp
import numpy as np
from jax import lax

D = 8192
QUERY_HEADS = 64
KEY_VALUE_HEADS = 8
HEAD_WIDTH = 128
TOKENS_PER_SHARD = 512
QUERY_PER_KV = 8
PACKED_TOKENS = 4096
OWNERS = 8
QB = 64
NDOC = 4
MAXLEN = 2048
N_TP = 4


def draw_rotated_keys(key, part):
    key = jax.random.fold_in(key, 11)
    final_output = jnp.clip(jax.random.normal(key, (PACKED_TOKENS, KEY_VALUE_HEADS * HEAD_WIDTH), jnp.float32), -4.0, 4.0)
    return final_output.astype(jnp.bfloat16)


def draw_rotated_queries(key, part):
    key = jax.random.fold_in(key, 23)
    final_output = jnp.clip(jax.random.normal(key, (PACKED_TOKENS, QUERY_HEADS * HEAD_WIDTH), jnp.float32), -4.0, 4.0)
    return final_output.astype(jnp.bfloat16)


def block_scale(rng, dims, pieces, low, top_value):
    def one(axis_at, shards_of):
        draws = jax.random.uniform(jax.random.fold_in(jax.random.fold_in(rng, 6), axis_at), (shards_of,), jnp.float32, low / len(pieces), top_value / len(pieces))
        return jnp.repeat(jnp.exp(draws), dims[axis_at] // shards_of).reshape((-1,) + (1,) * (len(dims) - axis_at - 1))

    level = one(*pieces[0])
    for cut in pieces[1:]:
        level = level * one(*cut)
    return level


def profile(count, total, limit, skew):
    loads = [(1 << 20) // math.isqrt(grade ** skew) + 1 for grade in range(2, count + 1)]
    surplus, given = total - limit - (count - 1), [1] * (count - 1)
    while surplus > 0:
        free = [i for i in range(count - 1) if given[i] < limit]
        pool, budget = sum([loads[i] for i in free]), surplus
        for i in free:
            more = min(limit - given[i], max(1, budget * loads[i] // pool), surplus)
            given[i] = given[i] + more
            surplus = surplus - more
    return np.array([limit] + given)


def uneven(key, count, total, reach, skew):
    if count == 2:
        one = jax.random.randint(key, (), max(1, total - reach), min(reach, total - 1) + 1)
        return jnp.stack([one, total - one])
    sizes = jnp.asarray(profile(count, total, reach, skew), jnp.int32)
    pairs = (count - 1) // 2
    donor, sink = sizes[1:1 + 2 * pairs:2], sizes[2:2 + 2 * pairs:2]
    room = jnp.minimum(donor - 1, reach - sink)
    moved = jax.random.randint(jax.random.fold_in(key, 1), (pairs,), 0, 1 << 20) % (room + 1)
    sizes = sizes.at[1:1 + 2 * pairs:2].set(donor - moved).at[2:2 + 2 * pairs:2].set(sink + moved)
    return sizes[jax.random.permutation(jax.random.fold_in(key, 2), count)]


def normal_values(key, dims, deviation, reach, pieces=(), held_as=jnp.bfloat16):
    array = deviation * jax.random.normal(key, dims, jnp.float32)
    if pieces:
        array = array * block_scale(key, dims, pieces, -0.22, 0.18)
    return jnp.clip(array, -reach, reach).astype(held_as)


def setup_inputs(seed: int = 0) -> dict:
    splits = jax.random.split(jax.random.key(seed), 7)
    return {
        "rotated_queries": draw_rotated_queries(jax.random.fold_in(splits[6], 71), 0),
        "rotated_keys": draw_rotated_keys(jax.random.fold_in(splits[6], 71), 0),
        "value_matrix": normal_values(splits[2], (PACKED_TOKENS, KEY_VALUE_HEADS * HEAD_WIDTH), 1.0, 6.0, ((0, 8), (1, 4))),
        "out_weight": normal_values(splits[3], (QUERY_HEADS * HEAD_WIDTH, D), (QUERY_HEADS * HEAD_WIDTH) ** -0.5, 0.0625, ((0, 4), (1, 8))),
        "doc_ids": jnp.searchsorted(jnp.cumsum(uneven(splits[4], NDOC, PACKED_TOKENS, MAXLEN, 2)), jnp.arange(PACKED_TOKENS), side="right").astype(jnp.int32),
        "assignment": jax.vmap(lambda own: jax.random.permutation(own, OWNERS))(jax.random.split(splits[5], OWNERS)).reshape((OWNERS, OWNERS)).astype(jnp.int32),
    }


def reference(rotated_queries, rotated_keys, value_matrix, out_weight, doc_ids, assignment):
    scale = 1.0 / math.sqrt(HEAD_WIDTH)
    positions = jnp.arange(PACKED_TOKENS, dtype=jnp.int32)
    number_blocks = PACKED_TOKENS // TOKENS_PER_SHARD
    query_tensor_five = rotated_queries.reshape(number_blocks, TOKENS_PER_SHARD, KEY_VALUE_HEADS, QUERY_PER_KV, HEAD_WIDTH)
    key_tensor_three = rotated_keys.astype(jnp.float32).reshape(PACKED_TOKENS, KEY_VALUE_HEADS, HEAD_WIDTH)
    value_tensor_three = value_matrix.astype(jnp.float32).reshape(PACKED_TOKENS, KEY_VALUE_HEADS, HEAD_WIDTH)

    def head_split(head_index):
        head_keys = lax.dynamic_index_in_dim(key_tensor_three, head_index, 1, keepdims=False)
        head_values = lax.dynamic_index_in_dim(value_tensor_three, head_index, 1, keepdims=False)

        def per_block(block_index):
            block_queries = query_tensor_five[block_index, :, head_index].astype(jnp.float32)
            block_pos = block_index * TOKENS_PER_SHARD + jnp.arange(TOKENS_PER_SHARD, dtype=jnp.int32)
            block_doc = lax.dynamic_slice_in_dim(doc_ids, block_index * TOKENS_PER_SHARD, TOKENS_PER_SHARD)
            scores = jnp.einsum('tgd,sd->tgs', block_queries, head_keys) * scale
            visible = (block_doc[:, None] == doc_ids[None, :]) & (positions[None, :] <= block_pos[:, None])
            visible = visible[:, None, :]
            row_max = lax.optimization_barrier(jnp.max(jnp.where(visible, scores, -jnp.inf), axis=-1, keepdims=True))
            exp_terms = jnp.where(visible, jnp.exp(scores - row_max), 0.0)
            denominator = lax.optimization_barrier(jnp.sum(exp_terms, axis=-1))
            weights = lax.optimization_barrier(exp_terms.astype(jnp.bfloat16)).astype(jnp.float32)
            numerator = jnp.einsum('tgs,sd->tgd', weights, head_values)
            return (numerator / denominator[..., None]).astype(jnp.bfloat16)
        return lax.map(per_block, jnp.arange(number_blocks, dtype=jnp.int32))
    attention_output = lax.map(head_split, jnp.arange(KEY_VALUE_HEADS, dtype=jnp.int32))
    attention_output = jnp.transpose(attention_output, (1, 2, 0, 3, 4)).reshape(PACKED_TOKENS, QUERY_HEADS * HEAD_WIDTH)
    columns = QUERY_HEADS * HEAD_WIDTH // N_TP
    projected = jnp.zeros((PACKED_TOKENS, D), jnp.float32)
    for split_index in range(N_TP):
        product = jnp.dot(attention_output[:, split_index * columns:(split_index + 1) * columns], out_weight[split_index * columns:(split_index + 1) * columns], preferred_element_type=jnp.float32)
        projected = projected + lax.optimization_barrier(product.astype(jnp.bfloat16)).astype(jnp.float32)
    projected = projected.astype(jnp.bfloat16)
    source_base = jnp.arange(number_blocks, dtype=jnp.int32) * TOKENS_PER_SHARD
    order = source_base[None, :, None] + jnp.transpose(assignment)[:, :, None] * QB + jnp.arange(QB, dtype=jnp.int32)[None, None, :]
    return jnp.take(projected, order.reshape(-1).astype(jnp.int32), axis=0)
```

```python
import functools
import math

import jax
import jax.numpy as jnp
from jax import lax
from jax.experimental import pallas as pl
from jax.experimental.pallas import tpu as pltpu
from jax.sharding import PartitionSpec as P

HEAD_WIDTH = 128
KEY_TILE = 256
QUERY_PER_KV = 8
neg_large = -1e30


def attend_kernel(first, last, q_ref, k_ref, v_ref, start_ref, pos_ref, o_ref):
    block = pl.program_id(1)
    rows = q_ref.shape[0]
    group = q_ref.shape[1] // HEAD_WIDTH
    width = group * rows
    factor = math.log2(math.e) / math.sqrt(HEAD_WIDTH)
    q = jnp.concatenate(
        [q_ref[:, h * HEAD_WIDTH:(h + 1) * HEAD_WIDTH] for h in range(group)], axis=0
    )
    start, pos = start_ref[0], pos_ref[0]

    def tile(i, carried):
        m, total, acc = carried
        base = pl.multiple_of(i * KEY_TILE, KEY_TILE)
        k = k_ref[pl.ds(base, KEY_TILE), :]
        v = v_ref[pl.ds(base, KEY_TILE), :]
        s = lax.dot_general(k, q, (((1,), (1,)), ((), ())), preferred_element_type=jnp.float32)
        key_pos = base + lax.broadcasted_iota(jnp.int32, (KEY_TILE, width), 0)
        s = jnp.where((key_pos >= start) & (key_pos <= pos), s, neg_large)
        new_m = jnp.maximum(m, jnp.max(s, axis=0, keepdims=True))
        alpha = jnp.exp2((m - new_m) * factor)
        p = jnp.exp2((s - new_m) * factor)
        total = total * alpha + jnp.sum(p, axis=0, keepdims=True)
        acc = acc * alpha + lax.dot_general(
            v, p.astype(jnp.bfloat16), (((0,), (0,)), ((), ())), preferred_element_type=jnp.float32
        )
        return new_m, total, acc

    m, total, acc = lax.fori_loop(
        first[block],
        last[block],
        tile,
        (
            jnp.full((1, width), neg_large, jnp.float32),
            jnp.zeros((1, width), jnp.float32),
            jnp.zeros((HEAD_WIDTH, width), jnp.float32),
        ),
    )
    out = (acc / total).T.astype(jnp.bfloat16)
    for h in range(group):
        o_ref[:, h * HEAD_WIDTH:(h + 1) * HEAD_WIDTH] = out[h * rows:(h + 1) * rows]


def attend(queries, block_pos, keys, values, doc_ids, block_rows):
    tokens_here, width = queries.shape
    blocks = tokens_here // block_rows
    kv_heads = keys.shape[1] // HEAD_WIDTH
    group = width // keys.shape[1]
    key_count = keys.shape[0]
    pos = block_pos[:, None] + jnp.arange(block_rows, dtype=jnp.int32)[None, :]
    query_doc = jnp.take(doc_ids, pos)
    start = jnp.sum((doc_ids[None, None, :] < query_doc[:, :, None]).astype(jnp.int32), axis=-1)
    first = start[:, 0] // KEY_TILE
    last = (block_pos + block_rows + KEY_TILE - 1) // KEY_TILE
    start_rows = jnp.tile(start, (1, group))[:, None, :]
    pos_rows = jnp.tile(pos, (1, group))[:, None, :]
    spec = pl.BlockSpec((block_rows, group * HEAD_WIDTH), lambda g, j, *_: (j, g))
    whole = pl.BlockSpec((key_count, HEAD_WIDTH), lambda g, j, *_: (0, g))
    row = pl.BlockSpec((1, 1, group * block_rows), lambda g, j, *_: (j, 0, 0))
    flops = 4 * tokens_here * width * key_count // 4
    return pl.pallas_call(
        attend_kernel,
        out_shape=jax.ShapeDtypeStruct((tokens_here, width), jnp.bfloat16),
        grid_spec=pltpu.PrefetchScalarGridSpec(
            num_scalar_prefetch=2,
            grid=(kv_heads, blocks),
            in_specs=[spec, whole, whole, row, row],
            out_specs=spec,
        ),
        compiler_params=pltpu.CompilerParams(vmem_limit_bytes=32 * 2**20),
        cost_estimate=pl.CostEstimate(
            flops=flops, bytes_accessed=4 * tokens_here * width, transcendentals=flops // 512
        ),
    )(first, last, queries, keys, values, start_rows, pos_rows)


def shards(rotated_queries, rotated_keys, value_matrix, out_weight, doc_ids, assignment):
    owners = lax.axis_size("ctx")
    owner_index = lax.axis_index("ctx")
    tokens_here = rotated_queries.shape[0]
    block_rows = tokens_here // owners
    width = rotated_queries.shape[1]
    my_row = lax.dynamic_index_in_dim(assignment, owner_index, 0, keepdims=False)
    my_column = lax.dynamic_index_in_dim(assignment, owner_index, 1, keepdims=False)
    source_base = jnp.arange(owners, dtype=jnp.int32) * tokens_here
    outgoing = jnp.take(rotated_queries.reshape(owners, block_rows, width), my_row, axis=0)
    arrived = lax.all_to_all(outgoing, "ctx", split_axis=0, concat_axis=0, tiled=True)
    keys = lax.all_gather(rotated_keys, "ctx", axis=0, tiled=True)
    values = lax.all_gather(value_matrix, "ctx", axis=0, tiled=True)
    weight = lax.all_gather(out_weight, "ctx", axis=1, tiled=True)
    attended = attend(
        arrived.reshape(tokens_here, width),
        source_base + my_column * block_rows,
        keys,
        values,
        doc_ids,
        block_rows,
    )
    partial_sums = jnp.dot(attended, weight, preferred_element_type=jnp.float32)
    return lax.psum_scatter(
        partial_sums.astype(jnp.bfloat16), "tp", scatter_dimension=1, tiled=True
    )


def solution(mesh):
    placed = (P("ctx", "tp"), P("ctx", "tp"), P("ctx", "tp"), P("tp", "ctx"), P(), P())
    return jax.shard_map(
        shards, mesh=mesh, in_specs=placed, out_specs=P("ctx", "tp"), check_vma=False
    )
```

```python
import functools
import math

import jax
import jax.numpy as jnp
from jax import lax
from jax.experimental import pallas as pl
from jax.experimental.pallas import tpu as pltpu
from jax.sharding import PartitionSpec as P

HEAD_WIDTH = 128
KEY_TILE = 256
neg_large = -1e30


def attend_kernel(first, last, q_ref, k_ref, v_ref, start_ref, pos_ref, o_ref):
    block = pl.program_id(1)
    rows = q_ref.shape[0]
    group = q_ref.shape[1] // HEAD_WIDTH
    width = group * rows
    factor = math.log2(math.e) / math.sqrt(HEAD_WIDTH)
    q = jnp.concatenate(
        [q_ref[:, h * HEAD_WIDTH:(h + 1) * HEAD_WIDTH] for h in range(group)], axis=0
    )
    start, pos = start_ref[0], pos_ref[0]

    def tile(i, carried):
        m, total, acc = carried
        base = pl.multiple_of(i * KEY_TILE, KEY_TILE)
        k = k_ref[pl.ds(base, KEY_TILE), :]
        v = v_ref[pl.ds(base, KEY_TILE), :]
        s = lax.dot_general(k, q, (((1,), (1,)), ((), ())), preferred_element_type=jnp.float32)
        key_pos = base + lax.broadcasted_iota(jnp.int32, (KEY_TILE, width), 0)
        s = jnp.where((key_pos >= start) & (key_pos <= pos), s, neg_large)
        new_m = jnp.maximum(m, jnp.max(s, axis=0, keepdims=True))
        alpha = jnp.exp2((m - new_m) * factor)
        p = jnp.exp2((s - new_m) * factor)
        total = total * alpha + jnp.sum(p, axis=0, keepdims=True)
        acc = acc * alpha + lax.dot_general(
            v, p.astype(jnp.bfloat16), (((0,), (0,)), ((), ())), preferred_element_type=jnp.float32
        )
        return new_m, total, acc

    m, total, acc = lax.fori_loop(
        first[block],
        last[block],
        tile,
        (
            jnp.full((1, width), neg_large, jnp.float32),
            jnp.zeros((1, width), jnp.float32),
            jnp.zeros((HEAD_WIDTH, width), jnp.float32),
        ),
    )
    out = (acc / total).T.astype(jnp.bfloat16)
    for h in range(group):
        o_ref[:, h * HEAD_WIDTH:(h + 1) * HEAD_WIDTH] = out[h * rows:(h + 1) * rows]


def attend(queries, block_pos, keys_values, kv_width, doc_ids, block_rows):
    tokens_here, width = queries.shape
    blocks = tokens_here // block_rows
    kv_heads = kv_width // HEAD_WIDTH
    group = width // kv_width
    key_count = keys_values.shape[0]
    pos = block_pos[:, None] + jnp.arange(block_rows, dtype=jnp.int32)[None, :]
    query_doc = jnp.take(doc_ids, pos)
    start = jnp.sum((doc_ids[None, None, :] < query_doc[:, :, None]).astype(jnp.int32), axis=-1)
    first = start[:, 0] // KEY_TILE
    last = (block_pos + block_rows + KEY_TILE - 1) // KEY_TILE
    start_rows = jnp.tile(start, (1, group))[:, None, :]
    pos_rows = jnp.tile(pos, (1, group))[:, None, :]
    spec = pl.BlockSpec((block_rows, group * HEAD_WIDTH), lambda g, j, *_: (j, g))
    key_spec = pl.BlockSpec((key_count, HEAD_WIDTH), lambda g, j, *_: (0, g))
    value_spec = pl.BlockSpec((key_count, HEAD_WIDTH), lambda g, j, *_: (0, kv_heads + g))
    row = pl.BlockSpec((1, 1, group * block_rows), lambda g, j, *_: (j, 0, 0))
    flops = 4 * tokens_here * width * key_count // 4
    return pl.pallas_call(
        attend_kernel,
        out_shape=jax.ShapeDtypeStruct((tokens_here, width), jnp.bfloat16),
        grid_spec=pltpu.PrefetchScalarGridSpec(
            num_scalar_prefetch=2,
            grid=(kv_heads, blocks),
            in_specs=[spec, key_spec, value_spec, row, row],
            out_specs=spec,
        ),
        compiler_params=pltpu.CompilerParams(vmem_limit_bytes=32 * 2**20),
        cost_estimate=pl.CostEstimate(
            flops=flops, bytes_accessed=4 * tokens_here * width, transcendentals=flops // 512
        ),
    )(first, last, queries, keys_values, keys_values, start_rows, pos_rows)


def project_kernel(n, per, a_ref, w_ref, o_ref, w, acc, own, sent, from_left, from_right,
                   w_sem, send_sem, left_sem, right_sem):
    z = lax.axis_index("tp")
    rows = a_ref.shape[0]
    tile = min(256, rows)
    barrier = pltpu.get_barrier_semaphore()

    @pl.when(z > 0)
    def _():
        pl.semaphore_signal(barrier, inc=1, device_id={"tp": z - 1}, device_id_type=pl.DeviceIdType.MESH)

    @pl.when(z < n - 1)
    def _():
        pl.semaphore_signal(barrier, inc=1, device_id={"tp": z + 1}, device_id_type=pl.DeviceIdType.MESH)

    def fetch(t):
        piece = pl.ds(t * per, per)
        return pltpu.make_async_copy(w_ref.at[piece], w.at[piece], w_sem.at[t])

    def rightward(t):
        return pltpu.make_async_remote_copy(
            src_ref=sent.at[t], dst_ref=from_left.at[t], send_sem=send_sem.at[t],
            recv_sem=left_sem.at[t], device_id={"tp": jnp.minimum(z + 1, n - 1)}, device_id_type=pl.DeviceIdType.MESH)

    def leftward(t):
        return pltpu.make_async_remote_copy(
            src_ref=sent.at[t], dst_ref=from_right.at[t], send_sem=send_sem.at[t],
            recv_sem=right_sem.at[t], device_id={"tp": jnp.maximum(z - 1, 0)}, device_id_type=pl.DeviceIdType.MESH)

    def order(k):
        return lax.select(k % 2 == 0, n - 1 - k // 2, k // 2)

    def begin(k, _):
        fetch(order(k)).start()
        return 0

    lax.fori_loop(0, n, begin, 0)
    pl.semaphore_wait(barrier, (z > 0).astype(jnp.int32) + (z < n - 1).astype(jnp.int32))

    def step(k, _):
        t = order(k)
        fetch(t).wait()

        def product(target):
            def part(r, _):
                at = pl.ds(pl.multiple_of(r * tile, tile), tile)
                for i in range(per):
                    target[i, at, :] = jnp.dot(
                        a_ref[at, :], w[t * per + i], preferred_element_type=jnp.float32
                    )
                return 0

            lax.fori_loop(0, rows // tile, part, 0)

        @pl.when(t == z)
        def _():
            product(own)

        @pl.when(t != z)
        def _():
            product(acc)

        @pl.when(t > z)
        def _():
            @pl.when(z > 0)
            def _():
                rightward(t).wait_recv()
                sent[t] = (acc[...] + from_left[t].astype(jnp.float32)).astype(jnp.bfloat16)

            @pl.when(z == 0)
            def _():
                sent[t] = acc[...].astype(jnp.bfloat16)

            rightward(t).start()

        @pl.when(t < z)
        def _():
            @pl.when(z < n - 1)
            def _():
                leftward(t).wait_recv()
                sent[t] = (acc[...] + from_right[t].astype(jnp.float32)).astype(jnp.bfloat16)

            @pl.when(z == n - 1)
            def _():
                sent[t] = acc[...].astype(jnp.bfloat16)

            leftward(t).start()

        return 0

    lax.fori_loop(0, n, step, 0)

    @pl.when(z > 0)
    def _():
        rightward(z).wait_recv()
        own[...] += from_left[z].astype(jnp.float32)

    @pl.when(z < n - 1)
    def _():
        leftward(z).wait_recv()
        own[...] += from_right[z].astype(jnp.float32)

    o_ref[...] = own[...].astype(jnp.bfloat16)

    def finish(t, _):
        @pl.when(t > z)
        def _():
            rightward(t).wait_send()

        @pl.when(t < z)
        def _():
            leftward(t).wait_send()

        return 0

    lax.fori_loop(0, n, finish, 0)


def project(attended, weight, n):
    owners, depth, columns = weight.shape
    rows = attended.shape[0]
    per = owners // n
    slots = pltpu.VMEM((n, per, rows, columns), jnp.bfloat16)
    sums = pltpu.VMEM((per, rows, columns), jnp.float32)
    return pl.pallas_call(
        functools.partial(project_kernel, n, per),
        out_shape=jax.ShapeDtypeStruct((per, rows, columns), jnp.bfloat16),
        in_specs=[pl.BlockSpec(memory_space=pltpu.VMEM), pl.BlockSpec(memory_space=pl.ANY)],
        out_specs=pl.BlockSpec(memory_space=pltpu.VMEM),
        scratch_shapes=[
            pltpu.VMEM(weight.shape, jnp.bfloat16), sums, sums, slots, slots, slots,
        ] + [pltpu.SemaphoreType.DMA((n,))] * 4,
        compiler_params=pltpu.CompilerParams(
            collective_id=0, has_side_effects=True, vmem_limit_bytes=48 * 2**20
        ),
        cost_estimate=pl.CostEstimate(
            flops=2 * rows * depth * owners * columns,
            bytes_accessed=2 * owners * depth * columns,
            transcendentals=0,
        ),
    )(attended, weight)


CHUNKS = 4


def shards(rotated_queries, rotated_keys, value_matrix, out_weight, doc_ids, assignment):
    owners = lax.axis_size("ctx")
    tp = lax.axis_size("tp")
    owner_index = lax.axis_index("ctx")
    tokens_here = rotated_queries.shape[0]
    block_rows = tokens_here // owners
    width = rotated_queries.shape[1]
    kv_width = rotated_keys.shape[1]
    my_row = lax.dynamic_index_in_dim(assignment, owner_index, 0, keepdims=False)
    my_column = lax.dynamic_index_in_dim(assignment, owner_index, 1, keepdims=False)
    source_base = jnp.arange(owners, dtype=jnp.int32) * tokens_here
    outgoing = jnp.take(rotated_queries.reshape(owners, block_rows, width), my_row, axis=0)
    arrived = lax.all_to_all(outgoing, "ctx", split_axis=0, concat_axis=0, tiled=True)
    keys_values = lax.all_gather(
        jnp.concatenate([rotated_keys, value_matrix], axis=1), "ctx", axis=0, tiled=True
    )
    columns = out_weight.shape[1] // CHUNKS
    weights = [
        lax.all_gather(out_weight[:, i * columns:(i + 1) * columns], "ctx", axis=0, tiled=False)
        for i in range(CHUNKS)
    ]
    attended = attend(
        arrived.reshape(tokens_here, width),
        source_base + my_column * block_rows,
        keys_values,
        kv_width,
        doc_ids,
        block_rows,
    )
    parts = [project(attended, weight, tp) for weight in weights]
    whole = jnp.concatenate(parts, axis=2)
    return jnp.concatenate([whole[i] for i in range(whole.shape[0])], axis=1)


def solution(mesh):
    placed = (P("ctx", "tp"), P("ctx", "tp"), P("ctx", "tp"), P("tp", "ctx"), P(), P())
    return jax.shard_map(
        shards, mesh=mesh, in_specs=placed, out_specs=P("ctx", "tp"), check_vma=False
    )
```

```python
import functools
import math

import jax
import jax.numpy as jnp
from jax import lax
from jax.experimental import pallas as pl
from jax.experimental.pallas import tpu as pltpu
from jax.sharding import PartitionSpec as P

HEAD_WIDTH = 128
KEY_TILE = 256
neg_large = -1e30


def attend_kernel(first, last, q_ref, k_ref, v_ref, start_ref, pos_ref, o_ref):
    block = pl.program_id(1)
    rows = q_ref.shape[0]
    group = q_ref.shape[1] // HEAD_WIDTH
    width = group * rows
    factor = math.log2(math.e) / math.sqrt(HEAD_WIDTH)
    q = jnp.concatenate(
        [q_ref[:, h * HEAD_WIDTH:(h + 1) * HEAD_WIDTH] for h in range(group)], axis=0
    )
    start, pos = start_ref[0], pos_ref[0]

    def tile(i, carried):
        m, total, acc = carried
        base = pl.multiple_of(i * KEY_TILE, KEY_TILE)
        k = k_ref[pl.ds(base, KEY_TILE), :]
        v = v_ref[pl.ds(base, KEY_TILE), :]
        s = lax.dot_general(k, q, (((1,), (1,)), ((), ())), preferred_element_type=jnp.float32)
        key_pos = base + lax.broadcasted_iota(jnp.int32, (KEY_TILE, width), 0)
        s = jnp.where((key_pos >= start) & (key_pos <= pos), s, neg_large)
        new_m = jnp.maximum(m, jnp.max(s, axis=0, keepdims=True))
        alpha = jnp.exp2((m - new_m) * factor)
        p = jnp.exp2((s - new_m) * factor)
        total = total * alpha + jnp.sum(p, axis=0, keepdims=True)
        acc = acc * alpha + lax.dot_general(
            v, p.astype(jnp.bfloat16), (((0,), (0,)), ((), ())), preferred_element_type=jnp.float32
        )
        return new_m, total, acc

    m, total, acc = lax.fori_loop(
        first[block],
        last[block],
        tile,
        (
            jnp.full((1, width), neg_large, jnp.float32),
            jnp.zeros((1, width), jnp.float32),
            jnp.zeros((HEAD_WIDTH, width), jnp.float32),
        ),
    )
    out = (acc / total).T.astype(jnp.bfloat16)
    for h in range(group):
        o_ref[:, h * HEAD_WIDTH:(h + 1) * HEAD_WIDTH] = out[h * rows:(h + 1) * rows]


def attend(queries, block_pos, keys_values, kv_width, doc_ids, block_rows):
    tokens_here, width = queries.shape
    blocks = tokens_here // block_rows
    kv_heads = kv_width // HEAD_WIDTH
    group = width // kv_width
    key_count = keys_values.shape[0]
    pos = block_pos[:, None] + jnp.arange(block_rows, dtype=jnp.int32)[None, :]
    query_doc = jnp.take(doc_ids, pos)
    start = jnp.sum((doc_ids[None, None, :] < query_doc[:, :, None]).astype(jnp.int32), axis=-1)
    first = start[:, 0] // KEY_TILE
    last = (block_pos + block_rows + KEY_TILE - 1) // KEY_TILE
    start_rows = jnp.tile(start, (1, group))[:, None, :]
    pos_rows = jnp.tile(pos, (1, group))[:, None, :]
    spec = pl.BlockSpec((block_rows, group * HEAD_WIDTH), lambda g, j, *_: (j, g))
    key_spec = pl.BlockSpec((key_count, HEAD_WIDTH), lambda g, j, *_: (0, g))
    value_spec = pl.BlockSpec((key_count, HEAD_WIDTH), lambda g, j, *_: (0, kv_heads + g))
    row = pl.BlockSpec((1, 1, group * block_rows), lambda g, j, *_: (j, 0, 0))
    flops = 4 * tokens_here * width * key_count // 4
    return pl.pallas_call(
        attend_kernel,
        out_shape=jax.ShapeDtypeStruct((tokens_here, width), jnp.bfloat16),
        grid_spec=pltpu.PrefetchScalarGridSpec(
            num_scalar_prefetch=2,
            grid=(kv_heads, blocks),
            in_specs=[spec, key_spec, value_spec, row, row],
            out_specs=spec,
        ),
        compiler_params=pltpu.CompilerParams(vmem_limit_bytes=32 * 2**20),
        cost_estimate=pl.CostEstimate(
            flops=flops, bytes_accessed=4 * tokens_here * width, transcendentals=flops // 512
        ),
    )(first, last, queries, keys_values, keys_values, start_rows, pos_rows)


def project_kernel(n, owners, a_ref, first_ref, weight_ref, o_ref, gathered, w, acc, own, sent,
                   from_left, from_right, w_sem, local_sem, gather_send, gather_recv, send_sem,
                   left_sem, right_sem):
    z, me = lax.axis_index("tp"), lax.axis_index("ctx")
    rows = a_ref.shape[0]
    columns = weight_ref.shape[1]
    depth = weight_ref.shape[0]
    chunks, half = columns // CHUNK, depth // 2
    per = owners // n
    tile = min(256, rows)
    paired = owners == 8
    twin = me + 1 - 2 * (me % 2)
    beside = me + 2 - 4 * ((me // 2) % 2)
    above = me + 4 - 8 * ((me // 4) % 2) if paired else me
    across = above + 2 - 4 * ((above // 2) % 2)
    partners = [beside, above, twin] if paired else [(me + i) % owners for i in range(1, owners)]

    barrier = pltpu.get_barrier_semaphore()

    def greet(device):
        pl.semaphore_signal(barrier, inc=1, device_id=device, device_id_type=pl.DeviceIdType.MESH)

    @pl.when(z > 0)
    def _():
        greet({"tp": jnp.maximum(z - 1, 0)})

    @pl.when(z < n - 1)
    def _():
        greet({"tp": jnp.minimum(z + 1, n - 1)})

    for partner in partners:
        greet({"ctx": partner})

    def pass_on(k, owner, piece, target, sid, mine=False):
        part = pl.ds(0, depth) if piece is None else pl.ds(piece * half, half)
        if mine:
            src = weight_ref.at[part, pl.ds(pl.multiple_of(k * CHUNK, CHUNK), CHUNK)]
        else:
            src = gathered.at[k, owner, part]
        return pltpu.make_async_remote_copy(
            src_ref=src, dst_ref=gathered.at[k, owner, part],
            send_sem=gather_send.at[k, sid], recv_sem=gather_recv.at[k, owner, piece or 0],
            device_id={"ctx": target}, device_id_type=pl.DeviceIdType.MESH)

    def keep(k):
        return pltpu.make_async_copy(
            weight_ref.at[:, pl.ds(pl.multiple_of(k * CHUNK, CHUNK), CHUNK)],
            gathered.at[k, me], local_sem.at[k])

    def arrive(k, owner, piece):
        pass_on(k, owner, piece, partners[0], 0).wait_recv()

    def gather_begin(k):
        for sid, partner in enumerate(partners):
            pass_on(k, me, None, partner, sid, mine=True).start()
        keep(k).start()

    def relay(k, sid):
        owner, piece, target = {
            3: (beside, 0, above), 4: (above, 1, beside), 5: (beside, None, twin),
            6: (above, None, twin), 7: (across, 0, twin), 8: (across, 1, twin),
        }[sid]
        return pass_on(k, owner, piece, target, sid)

    def gather_relay(k):
        if paired:
            arrive(k, beside, None)
            relay(k, 3).start()
            relay(k, 5).start()
            arrive(k, above, None)
            relay(k, 4).start()
            relay(k, 6).start()

    def gather_end(k):
        if paired:
            arrive(k, across, 0)
            relay(k, 7).start()
            arrive(k, across, 1)
            relay(k, 8).start()
            other = [twin]
            for step in (2, 4):
                other += [o + step - 2 * step * ((o // step) % 2) for o in other]
            for owner in other[:3]:
                arrive(k, owner, None)
            arrive(k, other[3], 0)
            arrive(k, other[3], 1)
        else:
            for partner in partners:
                arrive(k, partner, None)
        keep(k).wait()

    def gather_finish(k):
        for sid, partner in enumerate(partners):
            pass_on(k, me, None, partner, sid, mine=True).wait_send()
        if paired:
            for sid in range(3, 9):
                relay(k, sid).wait_send()

    def order(j):
        return lax.select(j % 2 == 0, n - 1 - j // 2, j // 2)

    def fetch(k, j, source):
        t, slot = order(j), j % 2
        return [
            pltpu.make_async_copy(
                source.at[k, t * per + i],
                w.at[slot, :, pl.ds(i * CHUNK, CHUNK)], w_sem.at[slot, i])
            for i in range(per)
        ]

    def fetch_start(k, j):
        @pl.when(k < HEAD)
        def _():
            for copy in fetch(jnp.minimum(k, HEAD - 1), j, first_ref):
                copy.start()

        @pl.when(k >= HEAD)
        def _():
            for copy in fetch(k, j, gathered):
                copy.start()

    def rightward(k, t):
        return pltpu.make_async_remote_copy(
            src_ref=sent.at[k, t], dst_ref=from_left.at[k, t], send_sem=send_sem.at[k, t],
            recv_sem=left_sem.at[k, t], device_id={"tp": jnp.minimum(z + 1, n - 1)},
            device_id_type=pl.DeviceIdType.MESH)

    def leftward(k, t):
        return pltpu.make_async_remote_copy(
            src_ref=sent.at[k, t], dst_ref=from_right.at[k, t], send_sem=send_sem.at[k, t],
            recv_sem=right_sem.at[k, t], device_id={"tp": jnp.maximum(z - 1, 0)},
            device_id_type=pl.DeviceIdType.MESH)

    def product(target, slot):
        def part(r, _):
            at = pl.ds(pl.multiple_of(r * tile, tile), tile)
            target[at, :] = jnp.dot(a_ref[at, :], w[slot], preferred_element_type=jnp.float32)
            return 0

        lax.fori_loop(0, rows // tile, part, 0)

    def reduce_step(k, j):
        t = order(j)

        @pl.when(j + 1 < n)
        def _():
            fetch_start(k, j + 1)

        for copy in fetch(k, j, gathered):
            copy.wait()

        @pl.when(t == z)
        def _():
            product(own, j % 2)

        @pl.when(t != z)
        def _():
            product(acc, j % 2)

        @pl.when(t > z)
        def _():
            @pl.when(z > 0)
            def _():
                rightward(k, t).wait_recv()
                sent[k, t] = (acc[...] + from_left[k, t].astype(jnp.float32)).astype(jnp.bfloat16)

            @pl.when(z == 0)
            def _():
                sent[k, t] = acc[...].astype(jnp.bfloat16)

            rightward(k, t).start()

        @pl.when(t < z)
        def _():
            @pl.when(z < n - 1)
            def _():
                leftward(k, t).wait_recv()
                sent[k, t] = (acc[...] + from_right[k, t].astype(jnp.float32)).astype(jnp.bfloat16)

            @pl.when(z == n - 1)
            def _():
                sent[k, t] = acc[...].astype(jnp.bfloat16)

            leftward(k, t).start()

    def reduce_end(k):
        @pl.when(z > 0)
        def _():
            rightward(k, z).wait_recv()
            own[...] += from_left[k, z].astype(jnp.float32)

        @pl.when(z < n - 1)
        def _():
            leftward(k, z).wait_recv()
            own[...] += from_right[k, z].astype(jnp.float32)

        for i in range(per):
            o_ref[:, pl.ds(pl.multiple_of(i * columns + k * CHUNK, CHUNK), CHUNK)] = own[
                :, i * CHUNK:(i + 1) * CHUNK
            ].astype(jnp.bfloat16)

    pl.semaphore_wait(
        barrier, (z > 0).astype(jnp.int32) + (z < n - 1).astype(jnp.int32) + len(partners)
    )
    for k in range(HEAD, min(HEAD + 1, chunks)):
        gather_begin(k)

    def chunk(k, _):
        @pl.when((k >= HEAD - 1) & (k + 2 < chunks))
        def _():
            gather_begin(k + 2)

        fetch_start(k, 0)

        def step(j, _):
            reduce_step(k, j)
            return 0

        lax.fori_loop(0, n, step, 0)

        @pl.when((k + 1 >= HEAD) & (k + 1 < chunks))
        def _():
            gather_relay(k + 1)

        reduce_end(k)

        @pl.when((k + 1 >= HEAD) & (k + 1 < chunks))
        def _():
            gather_end(k + 1)

        return 0

    lax.fori_loop(0, chunks, chunk, 0)

    def finish(k, _):
        def one(t, _):
            @pl.when(t > z)
            def _():
                rightward(k, t).wait_send()

            @pl.when(t < z)
            def _():
                leftward(k, t).wait_send()

            return 0

        lax.fori_loop(0, n, one, 0)

        @pl.when(k >= HEAD)
        def _():
            gather_finish(k)

        return 0

    lax.fori_loop(0, chunks, finish, 0)


def project(attended, first, weight, owners, n):
    rows = attended.shape[0]
    depth, columns = weight.shape
    chunks = columns // CHUNK
    per = owners // n
    wide = per * CHUNK
    slots = pltpu.VMEM((chunks, n, rows, wide), jnp.bfloat16)
    sums = pltpu.VMEM((rows, wide), jnp.float32)
    dma = pltpu.SemaphoreType.DMA
    out, _ = pl.pallas_call(
        functools.partial(project_kernel, n, owners),
        out_shape=(
            jax.ShapeDtypeStruct((rows, per * columns), jnp.bfloat16),
            jax.ShapeDtypeStruct((chunks, owners, depth, CHUNK), jnp.bfloat16),
        ),
        in_specs=[
            pl.BlockSpec(memory_space=pltpu.VMEM),
            pl.BlockSpec(memory_space=pl.ANY),
            pl.BlockSpec(memory_space=pl.ANY),
        ],
        out_specs=(pl.BlockSpec(memory_space=pltpu.VMEM), pl.BlockSpec(memory_space=pl.ANY)),
        scratch_shapes=[
            pltpu.VMEM((2, depth, wide), jnp.bfloat16), sums, sums, slots, slots, slots,
            dma((2, per)), dma((chunks,)), dma((chunks, max(9, owners))), dma((chunks, owners, 2)),
            dma((chunks, n)), dma((chunks, n)), dma((chunks, n)),
        ],
        compiler_params=pltpu.CompilerParams(
            collective_id=0, has_side_effects=True, vmem_limit_bytes=48 * 2**20
        ),
        cost_estimate=pl.CostEstimate(
            flops=2 * rows * depth * owners * columns,
            bytes_accessed=2 * owners * depth * columns,
            transcendentals=0,
        ),
    )(attended, first, weight)
    return out


CHUNK = 128
HEAD = 1


def shards(rotated_queries, rotated_keys, value_matrix, out_weight, doc_ids, assignment):
    owners = lax.axis_size("ctx")
    tp = lax.axis_size("tp")
    owner_index = lax.axis_index("ctx")
    tokens_here = rotated_queries.shape[0]
    block_rows = tokens_here // owners
    width = rotated_queries.shape[1]
    kv_width = rotated_keys.shape[1]
    my_row = lax.dynamic_index_in_dim(assignment, owner_index, 0, keepdims=False)
    my_column = lax.dynamic_index_in_dim(assignment, owner_index, 1, keepdims=False)
    source_base = jnp.arange(owners, dtype=jnp.int32) * tokens_here
    outgoing = jnp.take(rotated_queries.reshape(owners, block_rows, width), my_row, axis=0)
    arrived = lax.all_to_all(outgoing, "ctx", split_axis=0, concat_axis=0, tiled=True)
    keys_values = lax.all_gather(
        jnp.concatenate([rotated_keys, value_matrix], axis=1), "ctx", axis=0, tiled=True
    )
    first = jnp.stack([
        lax.all_gather(out_weight[:, i * CHUNK:(i + 1) * CHUNK], "ctx", axis=0, tiled=False)
        for i in range(HEAD)
    ])
    attended = attend(
        arrived.reshape(tokens_here, width),
        source_base + my_column * block_rows,
        keys_values,
        kv_width,
        doc_ids,
        block_rows,
    )
    return project(attended, first, out_weight, owners, tp)


def solution(mesh):
    placed = (P("ctx", "tp"), P("ctx", "tp"), P("ctx", "tp"), P("tp", "ctx"), P(), P())
    return jax.shard_map(
        shards, mesh=mesh, in_specs=placed, out_specs=P("ctx", "tp"), check_vma=False
    )
```

```python
import functools
import math

import jax
import jax.numpy as jnp
from jax import lax
from jax.experimental import pallas as pl
from jax.experimental.pallas import tpu as pltpu
from jax.sharding import PartitionSpec as P

HEAD_WIDTH = 128
KEY_TILE = 256
neg_large = -1e30


def attend_kernel(first, last, q_ref, k_ref, v_ref, start_ref, pos_ref, o_ref):
    block = pl.program_id(1)
    rows = q_ref.shape[0]
    group = q_ref.shape[1] // HEAD_WIDTH
    width = group * rows
    factor = math.log2(math.e) / math.sqrt(HEAD_WIDTH)
    q = jnp.concatenate(
        [q_ref[:, h * HEAD_WIDTH:(h + 1) * HEAD_WIDTH] for h in range(group)], axis=0
    )
    start, pos = start_ref[0], pos_ref[0]

    def tile(i, carried):
        m, total, acc = carried
        base = pl.multiple_of(i * KEY_TILE, KEY_TILE)
        k = k_ref[pl.ds(base, KEY_TILE), :]
        v = v_ref[pl.ds(base, KEY_TILE), :]
        s = lax.dot_general(k, q, (((1,), (1,)), ((), ())), preferred_element_type=jnp.float32)
        key_pos = base + lax.broadcasted_iota(jnp.int32, (KEY_TILE, width), 0)
        s = jnp.where((key_pos >= start) & (key_pos <= pos), s, neg_large)
        new_m = jnp.maximum(m, jnp.max(s, axis=0, keepdims=True))
        alpha = jnp.exp2((m - new_m) * factor)
        p = jnp.exp2((s - new_m) * factor)
        total = total * alpha + jnp.sum(p, axis=0, keepdims=True)
        acc = acc * alpha + lax.dot_general(
            v, p.astype(jnp.bfloat16), (((0,), (0,)), ((), ())), preferred_element_type=jnp.float32
        )
        return new_m, total, acc

    m, total, acc = lax.fori_loop(
        first[block],
        last[block],
        tile,
        (
            jnp.full((1, width), neg_large, jnp.float32),
            jnp.zeros((1, width), jnp.float32),
            jnp.zeros((HEAD_WIDTH, width), jnp.float32),
        ),
    )
    out = (acc / total).T.astype(jnp.bfloat16)
    for h in range(group):
        o_ref[:, h * HEAD_WIDTH:(h + 1) * HEAD_WIDTH] = out[h * rows:(h + 1) * rows]


def attend(queries, block_pos, keys_values, kv_width, doc_ids, block_rows):
    tokens_here, width = queries.shape
    blocks = tokens_here // block_rows
    kv_heads = kv_width // HEAD_WIDTH
    group = width // kv_width
    key_count = keys_values.shape[0]
    pos = block_pos[:, None] + jnp.arange(block_rows, dtype=jnp.int32)[None, :]
    query_doc = jnp.take(doc_ids, pos)
    start = jnp.sum((doc_ids[None, None, :] < query_doc[:, :, None]).astype(jnp.int32), axis=-1)
    first = start[:, 0] // KEY_TILE
    last = (block_pos + block_rows + KEY_TILE - 1) // KEY_TILE
    start_rows = jnp.tile(start, (1, group))[:, None, :]
    pos_rows = jnp.tile(pos, (1, group))[:, None, :]
    spec = pl.BlockSpec((block_rows, group * HEAD_WIDTH), lambda g, j, *_: (j, g))
    key_spec = pl.BlockSpec((key_count, HEAD_WIDTH), lambda g, j, *_: (0, g))
    value_spec = pl.BlockSpec((key_count, HEAD_WIDTH), lambda g, j, *_: (0, kv_heads + g))
    row = pl.BlockSpec((1, 1, group * block_rows), lambda g, j, *_: (j, 0, 0))
    flops = 4 * tokens_here * width * key_count // 4
    return pl.pallas_call(
        attend_kernel,
        out_shape=jax.ShapeDtypeStruct((tokens_here, width), jnp.bfloat16),
        grid_spec=pltpu.PrefetchScalarGridSpec(
            num_scalar_prefetch=2,
            grid=(kv_heads, blocks),
            in_specs=[spec, key_spec, value_spec, row, row],
            out_specs=spec,
        ),
        compiler_params=pltpu.CompilerParams(vmem_limit_bytes=32 * 2**20),
        cost_estimate=pl.CostEstimate(
            flops=flops, bytes_accessed=4 * tokens_here * width, transcendentals=flops // 512
        ),
    )(first, last, queries, keys_values, keys_values, start_rows, pos_rows)


def project_kernel(n, owners, a_ref, first_ref, weight_ref, o_ref, gathered, w, own, sent,
                   from_left, from_right, w_sem, local_sem, gather_send, gather_recv, send_sem,
                   left_sem, right_sem):
    z, me = lax.axis_index("tp"), lax.axis_index("ctx")
    rows = a_ref.shape[0]
    columns = weight_ref.shape[1]
    depth = weight_ref.shape[0]
    chunks, half = columns // CHUNK, depth // 2
    per = owners // n
    tile = min(256, rows)
    paired = owners == 8
    twin = me + 1 - 2 * (me % 2)
    beside = me + 2 - 4 * ((me // 2) % 2)
    above = me + 4 - 8 * ((me // 4) % 2) if paired else me
    across = above + 2 - 4 * ((above // 2) % 2)
    partners = [beside, above, twin] if paired else [(me + i) % owners for i in range(1, owners)]

    barrier = pltpu.get_barrier_semaphore()

    def greet(device):
        pl.semaphore_signal(barrier, inc=1, device_id=device, device_id_type=pl.DeviceIdType.MESH)

    @pl.when(z > 0)
    def _():
        greet({"tp": jnp.maximum(z - 1, 0)})

    @pl.when(z < n - 1)
    def _():
        greet({"tp": jnp.minimum(z + 1, n - 1)})

    for partner in partners:
        greet({"ctx": partner})

    def pass_on(k, owner, piece, target, sid, mine=False):
        part = pl.ds(0, depth) if piece is None else pl.ds(piece * half, half)
        if mine:
            src = weight_ref.at[part, pl.ds(pl.multiple_of(k * CHUNK, CHUNK), CHUNK)]
        else:
            src = gathered.at[k, owner, part]
        return pltpu.make_async_remote_copy(
            src_ref=src, dst_ref=gathered.at[k, owner, part],
            send_sem=gather_send.at[k, sid], recv_sem=gather_recv.at[k, owner, piece or 0],
            device_id={"ctx": target}, device_id_type=pl.DeviceIdType.MESH)

    def keep(k):
        return pltpu.make_async_copy(
            weight_ref.at[:, pl.ds(pl.multiple_of(k * CHUNK, CHUNK), CHUNK)],
            gathered.at[k, me], local_sem.at[k])

    def arrive(k, owner, piece):
        pass_on(k, owner, piece, partners[0], 0).wait_recv()

    def gather_begin(k):
        for sid, partner in enumerate(partners):
            pass_on(k, me, None, partner, sid, mine=True).start()
        keep(k).start()

    def relay(k, sid):
        owner, piece, target = {
            3: (beside, 0, above), 4: (above, 1, beside), 5: (beside, None, twin),
            6: (above, None, twin), 7: (across, 0, twin), 8: (across, 1, twin),
        }[sid]
        return pass_on(k, owner, piece, target, sid)

    def gather_relay(k):
        if paired:
            arrive(k, beside, None)
            relay(k, 3).start()
            relay(k, 5).start()
            arrive(k, above, None)
            relay(k, 4).start()
            relay(k, 6).start()

    def gather_end(k):
        if paired:
            arrive(k, across, 0)
            relay(k, 7).start()
            arrive(k, across, 1)
            relay(k, 8).start()
            other = [twin]
            for step in (2, 4):
                other += [o + step - 2 * step * ((o // step) % 2) for o in other]
            for owner in other[:3]:
                arrive(k, owner, None)
            arrive(k, other[3], 0)
            arrive(k, other[3], 1)
        else:
            for partner in partners:
                arrive(k, partner, None)
        keep(k).wait()

    def gather_finish(k):
        for sid, partner in enumerate(partners):
            pass_on(k, me, None, partner, sid, mine=True).wait_send()
        if paired:
            for sid in range(3, 9):
                relay(k, sid).wait_send()

    def order(j):
        return lax.select(j % 2 == 0, n - 1 - j // 2, j // 2)

    def fetch(k, j, source):
        t, slot = order(j), j % 2
        return [
            pltpu.make_async_copy(
                source.at[k, t * per + i],
                w.at[slot, :, pl.ds(i * CHUNK, CHUNK)], w_sem.at[slot, i])
            for i in range(per)
        ]

    def fetch_start(k, j):
        @pl.when(k < HEAD)
        def _():
            for copy in fetch(jnp.minimum(k, HEAD - 1), j, first_ref):
                copy.start()

        @pl.when(k >= HEAD)
        def _():
            for copy in fetch(k, j, gathered):
                copy.start()

    def rightward(k, t):
        return pltpu.make_async_remote_copy(
            src_ref=sent.at[k, t], dst_ref=from_left.at[k, t], send_sem=send_sem.at[k, t],
            recv_sem=left_sem.at[k, t], device_id={"tp": jnp.minimum(z + 1, n - 1)},
            device_id_type=pl.DeviceIdType.MESH)

    def leftward(k, t):
        return pltpu.make_async_remote_copy(
            src_ref=sent.at[k, t], dst_ref=from_right.at[k, t], send_sem=send_sem.at[k, t],
            recv_sem=right_sem.at[k, t], device_id={"tp": jnp.maximum(z - 1, 0)},
            device_id_type=pl.DeviceIdType.MESH)

    def product(k, t, slot):
        def part(r, _):
            at = pl.ds(pl.multiple_of(r * tile, tile), tile)
            sent[k, t, at, :] = jnp.dot(
                a_ref[at, :], w[slot], preferred_element_type=jnp.float32
            ).astype(jnp.bfloat16)
            return 0

        lax.fori_loop(0, rows // tile, part, 0)

    def multiply(k, j):
        t = order(j)

        @pl.when(j + 1 < n)
        def _():
            fetch_start(k, j + 1)

        for copy in fetch(k, j, gathered):
            copy.wait()
        product(k, t, j % 2)

        @pl.when((t > z) & (z == 0))
        def _():
            rightward(k, t).start()

        @pl.when((t < z) & (z == n - 1))
        def _():
            leftward(k, t).start()

    def add_on(k, t, other):
        sent[k, t] = (
            sent[k, t].astype(jnp.float32) + other[k, t].astype(jnp.float32)
        ).astype(jnp.bfloat16)

    def forward(i, j):
        t = order(j)
        k_right, k_left = i - z, i - (n - 1 - z)

        @pl.when((t > z) & (z > 0) & (k_right >= 0) & (k_right < chunks))
        def _():
            rightward(k_right, t).wait_recv()
            add_on(k_right, t, from_left)
            rightward(k_right, t).start()

        @pl.when((t < z) & (z < n - 1) & (k_left >= 0) & (k_left < chunks))
        def _():
            leftward(k_left, t).wait_recv()
            add_on(k_left, t, from_right)
            leftward(k_left, t).start()

    def reduce_end(k):
        own[...] = sent[k, z].astype(jnp.float32)

        @pl.when(z > 0)
        def _():
            rightward(k, z).wait_recv()
            own[...] += from_left[k, z].astype(jnp.float32)

        @pl.when(z < n - 1)
        def _():
            leftward(k, z).wait_recv()
            own[...] += from_right[k, z].astype(jnp.float32)

        for i in range(per):
            o_ref[:, pl.ds(pl.multiple_of(i * columns + k * CHUNK, CHUNK), CHUNK)] = own[
                :, i * CHUNK:(i + 1) * CHUNK
            ].astype(jnp.bfloat16)

    pl.semaphore_wait(
        barrier, (z > 0).astype(jnp.int32) + (z < n - 1).astype(jnp.int32) + len(partners)
    )
    for k in range(HEAD, min(HEAD + 1, chunks)):
        gather_begin(k)

    lag = jnp.maximum(z, n - 1 - z)

    def iteration(i, _):
        @pl.when((i + 1 >= HEAD) & (i + 1 < chunks))
        def _():
            gather_relay(i + 1)

        @pl.when((i >= HEAD - 1) & (i + 2 < chunks))
        def _():
            gather_begin(i + 2)

        @pl.when(i < chunks)
        def _():
            fetch_start(i, 0)

            def step(j, _):
                multiply(i, j)
                return 0

            lax.fori_loop(0, n, step, 0)

        def pass_step(j, _):
            forward(i, j)
            return 0

        lax.fori_loop(0, n, pass_step, 0)

        @pl.when((i + 1 >= HEAD) & (i + 1 < chunks))
        def _():
            gather_end(i + 1)

        @pl.when((i >= lag) & (i - lag < chunks))
        def _():
            reduce_end(i - lag)

        return 0

    lax.fori_loop(0, chunks + n - 1, iteration, 0)

    def finish(k, _):
        def one(t, _):
            @pl.when(t > z)
            def _():
                rightward(k, t).wait_send()

            @pl.when(t < z)
            def _():
                leftward(k, t).wait_send()

            return 0

        lax.fori_loop(0, n, one, 0)

        @pl.when(k >= HEAD)
        def _():
            gather_finish(k)

        return 0

    lax.fori_loop(0, chunks, finish, 0)


def project(attended, first, weight, owners, n):
    rows = attended.shape[0]
    depth, columns = weight.shape
    chunks = columns // CHUNK
    per = owners // n
    wide = per * CHUNK
    slots = pltpu.VMEM((chunks, n, rows, wide), jnp.bfloat16)
    sums = pltpu.VMEM((rows, wide), jnp.float32)
    dma = pltpu.SemaphoreType.DMA
    out, _ = pl.pallas_call(
        functools.partial(project_kernel, n, owners),
        out_shape=(
            jax.ShapeDtypeStruct((rows, per * columns), jnp.bfloat16),
            jax.ShapeDtypeStruct((chunks, owners, depth, CHUNK), jnp.bfloat16),
        ),
        in_specs=[
            pl.BlockSpec(memory_space=pltpu.VMEM),
            pl.BlockSpec(memory_space=pl.ANY),
            pl.BlockSpec(memory_space=pl.ANY),
        ],
        out_specs=(pl.BlockSpec(memory_space=pltpu.VMEM), pl.BlockSpec(memory_space=pl.ANY)),
        scratch_shapes=[
            pltpu.VMEM((2, depth, wide), jnp.bfloat16), sums, slots, slots, slots,
            dma((2, per)), dma((chunks,)), dma((chunks, max(9, owners))), dma((chunks, owners, 2)),
            dma((chunks, n)), dma((chunks, n)), dma((chunks, n)),
        ],
        compiler_params=pltpu.CompilerParams(
            collective_id=0, has_side_effects=True, vmem_limit_bytes=48 * 2**20
        ),
        cost_estimate=pl.CostEstimate(
            flops=2 * rows * depth * owners * columns,
            bytes_accessed=2 * owners * depth * columns,
            transcendentals=0,
        ),
    )(attended, first, weight)
    return out


CHUNK = 256
HEAD = 1


def shards(rotated_queries, rotated_keys, value_matrix, out_weight, doc_ids, assignment):
    owners = lax.axis_size("ctx")
    tp = lax.axis_size("tp")
    owner_index = lax.axis_index("ctx")
    tokens_here = rotated_queries.shape[0]
    block_rows = tokens_here // owners
    width = rotated_queries.shape[1]
    kv_width = rotated_keys.shape[1]
    my_row = lax.dynamic_index_in_dim(assignment, owner_index, 0, keepdims=False)
    my_column = lax.dynamic_index_in_dim(assignment, owner_index, 1, keepdims=False)
    source_base = jnp.arange(owners, dtype=jnp.int32) * tokens_here
    outgoing = jnp.take(rotated_queries.reshape(owners, block_rows, width), my_row, axis=0)
    arrived = lax.all_to_all(outgoing, "ctx", split_axis=0, concat_axis=0, tiled=True)
    keys_values = lax.all_gather(
        jnp.concatenate([rotated_keys, value_matrix], axis=1), "ctx", axis=0, tiled=True
    )
    first = jnp.stack([
        lax.all_gather(out_weight[:, i * CHUNK:(i + 1) * CHUNK], "ctx", axis=0, tiled=False)
        for i in range(HEAD)
    ])
    attended = attend(
        arrived.reshape(tokens_here, width),
        source_base + my_column * block_rows,
        keys_values,
        kv_width,
        doc_ids,
        block_rows,
    )
    return project(attended, first, out_weight, owners, tp)


def solution(mesh):
    placed = (P("ctx", "tp"), P("ctx", "tp"), P("ctx", "tp"), P("tp", "ctx"), P(), P())
    return jax.shard_map(
        shards, mesh=mesh, in_specs=placed, out_specs=P("ctx", "tp"), check_vma=False
    )
```
